32 devices in a mesh: dp: 8 (over z, y), fsdp: 4 (over x, core).
Axes of the slice: x: 2, y: 2, z: 4, core: 2. Of those that a mesh axis runs over, the one named last changes fastest.
Arguments:
- tokens: bfloat16 [4096, 1024], P(('dp', 'fsdp')), may hold values from -6 to 6
- cotangent: bfloat16 [4096, 1024], P(('dp', 'fsdp')), may hold values from -6 to 6
- routes: int32 [4096, 1], P(('dp', 'fsdp')), may hold values from 0 to 8; in each aligned block of 128 rows (0 to 127, 128 to 255, ...) at most 16 rows name the same one
- norm_gain_vector: float32 [1024], replicated, may hold values from 0.25 to 1.75
- up_weight: bfloat16 [1024, 4096], P(None, 'fsdp'), may hold values from -0.1875 to 0.1875
- up_bias: float32 [4096], P('fsdp'), may hold values from -4 to 4
- down_weight: bfloat16 [4096, 1024], P('fsdp'), may hold values from -0.09375 to 0.09375
Outputs:
- input_grad: bfloat16 [4096, 1024], P(('dp', 'fsdp'))
- up_grad: float32 [1024, 4096], P(None, 'fsdp')
- bias_grad: float32 [4096], P('fsdp')
- down_grad: float32 [4096, 1024], P('fsdp')
- gain_grad: float32 [1024], replicated
The draws below stay inside these ranges and needn't reach their ends.
Inputs may be any that keep to these rules, and one draw needn't show every extreme that they name: `routes`: among the 128 slots of one device no value below 8 appears more than 16 times; the value 8 marks a padding slot.
All inputs are finite; a program needn't handle non-finite values.
Results may differ from the reference program's by a relative error of at most 0.024.
Values may be sent and summed in bfloat16 or wider, within the bound.
No kernel may reach another device: no remote copies, remote signals or barrier semaphores. Data moves between devices by JAX's collectives and lax.ppermute only.
A program may use at most 128 MiB of HBM per device.

```python
import math
import jax
import jax.numpy as jnp
import numpy as np
from jax import lax

D = 1024
FF = 4096
ROWS = 128
CAP = 16
TOKENS = 4096
N_DP = 8
N_FSDP = 4


def block_scale(rng, dims, split, least, largest):
    gain = 1.0
    for dim, parts in split:
        steps = jax.random.uniform(jax.random.fold_in(jax.random.fold_in(rng, 6), dim), (parts,), jnp.float32, least / len(split), largest / len(split))
        gain = gain * jnp.repeat(jnp.exp(steps), dims[dim] // parts).reshape((-1,) + (1,) * (len(dims) - 1 - dim))
    return gain


def deal_out(rng, own, number, rows, number_of, top, reach, lean):
    order = jax.random.permutation(rng, number_of)
    heavy_load, ordinary = load_shares(number_of, rows * top, reach, lean, True), load_shares(number_of, rows * top, reach, lean, False)
    places = jnp.arange(number_of)

    def named(lengths, rotation):
        used = int((lengths > 0).sum())
        fixed = max(1, used // 4)
        shifted = fixed + (places - fixed + rotation * (used - fixed)) % max(1, number_of - fixed)
        return jnp.zeros((number_of,), jnp.int32).at[order[jnp.where(places < fixed, places, shifted)]].set(jnp.asarray(lengths, jnp.int32))

    lengths = jnp.where(number % 4 == 0, named(heavy_load, number // 4), named(ordinary, number - number // 4 - 1))
    mixed = jax.random.permutation(jax.random.fold_in(own, 3), number_of)
    giver, receiver = mixed[0:number_of // 2 * 2:2], mixed[1:number_of // 2 * 2:2]
    room = jnp.minimum(lengths[giver] - 1, reach - lengths[receiver]) // 2
    room = jnp.where((giver == order[0]) | (receiver == order[0]) | (lengths[receiver] == 0), 0, jnp.maximum(room, 0))
    shifted = jax.random.randint(jax.random.fold_in(own, 4), (number_of // 2,), 0, 1 << 20) % (room + 1)
    lengths = lengths.at[giver].add(-shifted).at[receiver].add(shifted)
    items = jnp.searchsorted(jnp.cumsum(lengths), jnp.arange(rows * top), side="right").astype(jnp.int32)
    grid = items.reshape(top, rows).T
    grid = grid[jax.random.permutation(jax.random.fold_in(own, 1), rows)]
    rotation = jax.random.randint(jax.random.fold_in(own, 2), (rows, 1), 0, top)
    return jnp.take_along_axis(grid, (jnp.arange(top)[None, :] + rotation) % top, axis=1)


def load_shares(number_of, total, reach, skew, full):
    portions = [(1 << 20) // math.isqrt(standing ** skew) + 1 for standing in range(1, number_of + 1)]
    largest = reach if full else min(reach, max(-(-total // number_of), total * portions[0] // sum(portions)))
    least = 1 if total - largest >= number_of - 1 else 0
    holding, spare = [largest] + [least] * (number_of - 1), total - largest - least * (number_of - 1)
    while spare > 0:
        free = [i for i in range(1, number_of) if holding[i] < largest] or [i for i in range(1, number_of) if holding[i] < reach]
        mass, remaining = sum([portions[i] for i in free]), spare
        for i in free:
            extra = min(reach - holding[i], max(1, remaining * portions[i] // mass), spare)
            holding[i] = holding[i] + extra
            spare = spare - extra
    return np.array(holding)


def normal_values(rng, dims, scale, bound, cuts=(), held_as=jnp.bfloat16):
    array = scale * jax.random.normal(rng, dims, jnp.float32)
    if cuts:
        array = array * block_scale(rng, dims, cuts, -0.22, 0.18)
    return jnp.clip(array, -bound, bound).astype(held_as)


def setup_inputs(seed: int = 0) -> dict:
    streams_of = jax.random.split(jax.random.key(seed), 8)
    tokens = normal_values(streams_of[0], (TOKENS, D), 1.0, 6.0, ((0, 32),))
    cotangent = normal_values(streams_of[1], (TOKENS, D), 1.0, 6.0, ((0, 32),))
    routes_keys = jax.random.split(jax.random.fold_in(streams_of[2], 1), TOKENS // ROWS)
    routes_turns = jax.random.permutation(jax.random.fold_in(streams_of[2], 3), TOKENS // ROWS)
    routes = jax.vmap(lambda own, number: deal_out(jax.random.fold_in(streams_of[2], 2), own, number, ROWS, N_DP + 1, 1, CAP, 2))(routes_keys, routes_turns).reshape((TOKENS, 1))
    norm_gain_vector = jnp.clip(1.0 + 0.15 * jax.random.normal(streams_of[3], (D,), jnp.float32), 0.25, 1.75)
    up_weight = normal_values(streams_of[4], (D, FF), D ** -0.5, 0.1875, ((1, 4),))
    up_bias = normal_values(streams_of[5], (FF,), 1.0, 4.0, ((0, 4),), jnp.float32)
    down_weight = normal_values(streams_of[6], (FF, D), FF ** -0.5, 0.09375, ((0, 4),))
    return dict(tokens=tokens, cotangent=cotangent, routes=routes, norm_gain_vector=norm_gain_vector, up_weight=up_weight, up_bias=up_bias, down_weight=down_weight)


root_two_pi = 0.7978845608
cubic = 0.044715

def gelu_pair(pre):
    inner = root_two_pi * (pre + cubic * pre * pre * pre)
    tangent = jnp.tanh(inner)
    act = 0.5 * pre * (1.0 + tangent)
    slope = 0.5 * (1.0 + tangent) + 0.5 * pre * (1.0 - tangent * tangent) * root_two_pi * (1.0 + 3.0 * cubic * pre * pre)
    return (act, slope)

def apply_layer_norm(values):
    row_average = lax.optimization_barrier(jnp.mean(values, axis=1, keepdims=True))
    centered = values - row_average
    variance = lax.optimization_barrier(jnp.mean(centered * centered, axis=1, keepdims=True))
    inverse_std = 1.0 / jnp.sqrt(variance + 1e-05)
    return (centered * inverse_std, inverse_std)

def reference(tokens, cotangent, routes, norm_gain_vector, up_weight, up_bias, down_weight):
    capacity = ROWS // N_DP
    target = routes[:, 0].reshape(N_DP, N_FSDP, ROWS)
    matches = (target[..., None] == jnp.arange(N_DP + 1, dtype=jnp.int32)).astype(jnp.int32)
    earlier = jnp.cumsum(matches, axis=2) - matches
    ranked = lax.optimization_barrier(jnp.sum(earlier * matches, axis=3)).astype(jnp.int32)
    source = jnp.broadcast_to(jnp.arange(N_DP, dtype=jnp.int32)[:, None, None], target.shape)
    column = jnp.broadcast_to(jnp.arange(N_FSDP, dtype=jnp.int32)[None, :, None], target.shape)
    place = (source * capacity + ranked).astype(jnp.int32)
    inputs4 = tokens.reshape(N_DP, N_FSDP, ROWS, D)
    cot4 = cotangent.reshape(N_DP, N_FSDP, ROWS, D)
    packed_in = jnp.zeros((N_DP, N_FSDP, ROWS, D), jnp.bfloat16).at[target, column, place].set(inputs4, mode='drop')
    packed_cot = jnp.zeros((N_DP, N_FSDP, ROWS, D), jnp.bfloat16).at[target, column, place].set(cot4, mode='drop')
    block = FF // N_FSDP

    def group(pair):
        group_input_rows, group_cotangent_rows = pair
        group_input_rows = group_input_rows.reshape(N_FSDP * ROWS, D)
        group_cotangent_rows = group_cotangent_rows.reshape(N_FSDP * ROWS, D)
        standardized_rows, inverse_std = apply_layer_norm(group_input_rows.astype(jnp.float32))
        normed_values = (standardized_rows * norm_gain_vector).astype(jnp.bfloat16)
        pre = jnp.dot(normed_values, up_weight, preferred_element_type=jnp.float32) + up_bias
        act_full, slope = gelu_pair(pre)
        act = act_full.astype(jnp.bfloat16)
        act_grad = jnp.dot(group_cotangent_rows, down_weight.T, preferred_element_type=jnp.float32)
        pre_grad = (act_grad * slope).astype(jnp.bfloat16)
        down_part = jnp.dot(act.T, group_cotangent_rows, preferred_element_type=jnp.float32)
        up_part = jnp.dot(normed_values.T, pre_grad, preferred_element_type=jnp.float32)
        bias_part = lax.optimization_barrier(jnp.sum(pre_grad.astype(jnp.float32), axis=0))
        normed_rows_gradient = jnp.zeros((N_FSDP * ROWS, D), jnp.float32)
        for index in range(N_FSDP):
            partial_term = jnp.dot(pre_grad[:, index * block:(index + 1) * block], up_weight[:, index * block:(index + 1) * block].T, preferred_element_type=jnp.float32)
            rounded = lax.optimization_barrier(partial_term.astype(jnp.bfloat16))
            normed_rows_gradient = normed_rows_gradient + rounded.astype(jnp.float32)
        partial_gain_grad = lax.optimization_barrier(jnp.sum(normed_rows_gradient * standardized_rows, axis=0))
        scaled_values = normed_rows_gradient * norm_gain_vector
        final_result = group_cotangent_rows.astype(jnp.float32) + inverse_std * (scaled_values - lax.optimization_barrier(jnp.mean(scaled_values, axis=1, keepdims=True)) - standardized_rows * lax.optimization_barrier(jnp.mean(scaled_values * standardized_rows, axis=1, keepdims=True)))
        return (final_result.astype(jnp.bfloat16), up_part, bias_part, down_part, partial_gain_grad)
    results, up_parts, bias_parts, down_parts, gain_parts = lax.map(group, (packed_in, packed_cot))
    input_grad = results.reshape(TOKENS, D)
    return (input_grad, lax.optimization_barrier(jnp.sum(up_parts, axis=0)), lax.optimization_barrier(jnp.sum(bias_parts, axis=0)), lax.optimization_barrier(jnp.sum(down_parts, axis=0)), lax.optimization_barrier(jnp.sum(gain_parts, axis=0)))
```

```python
import jax
import jax.numpy as jnp
from jax import lax
from jax.sharding import PartitionSpec as P

root_two_pi = 0.7978845608
cubic = 0.044715
f32 = jnp.float32
bf16 = jnp.bfloat16


def gelu_pair(pre):
    inner = root_two_pi * (pre + cubic * pre * pre * pre)
    tangent = jnp.tanh(inner)
    act = 0.5 * pre * (1.0 + tangent)
    slope = 0.5 * (1.0 + tangent) + 0.5 * pre * (1.0 - tangent * tangent) * root_two_pi * (
        1.0 + 3.0 * cubic * pre * pre
    )
    return (act, slope)


def apply_layer_norm(values):
    row_average = jnp.mean(values, axis=1, keepdims=True)
    centered = values - row_average
    variance = jnp.mean(centered * centered, axis=1, keepdims=True)
    inverse_std = 1.0 / jnp.sqrt(variance + 1e-05)
    return (centered * inverse_std, inverse_std)


def ring_order(n):
    if n % 2:
        return list(range(n))
    return list(range(0, n, 2)) + list(range(n - 1, 0, -2))


def butterfly_sum(value, axis):
    n = lax.axis_size(axis)
    if n & (n - 1):
        return lax.psum(value, axis)
    step = 1
    while step < n:
        value = value + lax.ppermute(value, axis, [(i, i ^ step) for i in range(n)])
        step *= 2
    return value


def shards(tokens, cotangent, routes, norm_gain_vector, up_weight, up_bias, down_weight):
    particle_slot_count, width = tokens.shape
    hidden = up_weight.shape[1]
    dp_size = lax.axis_size("dp")
    fsdp_size = lax.axis_size("fsdp")
    capacity = particle_slot_count // dp_size
    target = routes[:, 0]
    matches = (target[:, None] == jnp.arange(dp_size + 1, dtype=jnp.int32)[None, :]).astype(
        jnp.int32
    )
    earlier = jnp.cumsum(matches, axis=0) - matches
    ranked = jnp.sum(earlier * matches, axis=1)
    slot_index = jnp.where(target < dp_size, target * capacity + ranked, -1)
    placing = (
        slot_index[None, :] == jnp.arange(particle_slot_count, dtype=jnp.int32)[:, None]
    ).astype(bf16)
    send_in = jnp.dot(placing, tokens, preferred_element_type=f32).astype(bf16)
    send_cot = jnp.dot(placing, cotangent, preferred_element_type=f32).astype(bf16)
    packed_in, packed_cot = (
        lax.all_to_all(send_in, "dp", split_axis=0, concat_axis=0, tiled=True),
        lax.all_to_all(send_cot, "dp", split_axis=0, concat_axis=0, tiled=True),
    )
    gathered_input_rows = lax.all_gather(packed_in, "fsdp", axis=0, tiled=True)
    all_cot = lax.all_gather(packed_cot, "fsdp", axis=0, tiled=True)

    own_standardized, own_inverse = apply_layer_norm(packed_in.astype(f32))
    standardized, _ = apply_layer_norm(gathered_input_rows.astype(f32))
    normed = (standardized * norm_gain_vector).astype(bf16)
    pre = jnp.dot(normed, up_weight, preferred_element_type=f32) + up_bias
    act_full, slope = gelu_pair(pre)
    act = act_full.astype(bf16)
    act, slope = lax.optimization_barrier((act, slope))
    act_grad = jnp.einsum("rd,kd->rk", all_cot, down_weight, preferred_element_type=f32)
    pre_grad = (act_grad * slope).astype(bf16)

    order = ring_order(dp_size)
    position = [0] * dp_size
    for place, device in enumerate(order):
        position[device] = place
    here = jnp.array(position, jnp.int32)[lax.axis_index("dp")]
    forward = [(order[i], order[(i + 1) % dp_size]) for i in range(dp_size)]
    backward = [(order[i], order[i - 1]) for i in range(dp_size)]
    chains = []
    for lhs, rhs in ((act, all_cot), (normed, pre_grad)):
        columns = rhs.shape[1] // 2
        for way, perm in ((1, forward), (-1, backward)):
            half = rhs[:, :columns] if way > 0 else rhs[:, columns:]
            chains.append((lhs, half, way, perm))

    def own_part(chain, piece):
        lhs, half, _, _ = chain
        rows = lhs.shape[1] // dp_size
        block = lax.dynamic_slice_in_dim(lhs, (piece % dp_size) * rows, rows, 1)
        return lax.dot_general(
            block, half, (((0,), (0,)), ((), ())), preferred_element_type=f32
        )

    totals = [own_part(c, here - c[2]).astype(bf16) for c in chains]
    for step in range(dp_size - 1):
        for i, c in enumerate(chains):
            arrived = lax.ppermute(totals[i], "dp", c[3])
            part = own_part(c, here - c[2] * (step + 2))
            totals[i] = (arrived.astype(f32) + part).astype(bf16)
    results = [jnp.zeros((width, hidden), f32), jnp.zeros((hidden, width), f32)]

    def put(i, piece, values):
        which = 1 - i // 2
        columns = values.shape[1]
        results[which] = lax.dynamic_update_slice(
            results[which],
            values.astype(f32),
            ((piece % dp_size) * values.shape[0], columns * (i % 2)),
        )

    for i, c in enumerate(chains):
        put(i, here, totals[i])
    for step in range(dp_size - 1):
        for i, c in enumerate(chains):
            totals[i] = lax.ppermute(totals[i], "dp", c[3])
            put(i, here - c[2] * (step + 1), totals[i])
    up_grad, down_grad = results

    partial = jnp.einsum("rk,dk->rd", pre_grad, up_weight, preferred_element_type=f32).astype(bf16)
    mine = lax.axis_index("fsdp")

    def rows_of(owner):
        return lax.dynamic_slice_in_dim(
            partial, (owner % fsdp_size) * particle_slot_count, particle_slot_count, 0
        )

    normed_rows_gradient = rows_of(mine).astype(f32)
    for distance in range(1, fsdp_size):
        arrived = lax.ppermute(
            rows_of(mine + distance),
            "fsdp",
            [(i, (i + distance) % fsdp_size) for i in range(fsdp_size)],
        )
        normed_rows_gradient = normed_rows_gradient + arrived.astype(f32)

    bias_part = jnp.sum(pre_grad.astype(f32), axis=0)
    gain_part = jnp.sum(normed_rows_gradient * own_standardized, axis=0)
    gain_part = butterfly_sum(gain_part, "fsdp")
    small = butterfly_sum(jnp.concatenate([gain_part, bias_part]), "dp")
    gain_grad, bias_grad = small[:width], small[width:]
    scaled_values = normed_rows_gradient * norm_gain_vector
    final_result = packed_cot.astype(f32) + own_inverse * (
        scaled_values
        - jnp.mean(scaled_values, axis=1, keepdims=True)
        - own_standardized * jnp.mean(scaled_values * own_standardized, axis=1, keepdims=True)
    )
    return (final_result.astype(bf16), up_grad, bias_grad, down_grad, gain_grad)


def solution(mesh):
    return jax.shard_map(
        shards,
        mesh=mesh,
        in_specs=(
            P(("dp", "fsdp"), None),
            P(("dp", "fsdp"), None),
            P(("dp", "fsdp"), None),
            P(),
            P(None, "fsdp"),
            P("fsdp"),
            P("fsdp", None),
        ),
        out_specs=(P(("dp", "fsdp"), None), P(None, "fsdp"), P("fsdp"), P("fsdp", None), P()),
        check_vma=False,
    )
```

```python
import functools

import jax
import jax.numpy as jnp
from jax import lax
from jax.experimental import pallas as pl
from jax.experimental.pallas import tpu as pltpu
from jax.sharding import PartitionSpec as P

root_two_pi = 0.7978845608
cubic = 0.044715
f32 = jnp.float32
bf16 = jnp.bfloat16
VMEM = pl.BlockSpec(memory_space=pltpu.VMEM)


def gelu_pair(pre):
    inner = root_two_pi * (pre + cubic * pre * pre * pre)
    tangent = jnp.tanh(inner)
    act = 0.5 * pre * (1.0 + tangent)
    slope = 0.5 * (1.0 + tangent) + 0.5 * pre * (1.0 - tangent * tangent) * root_two_pi * (
        1.0 + 3.0 * cubic * pre * pre
    )
    return (act, slope)


def apply_layer_norm(values):
    row_average = jnp.mean(values, axis=1, keepdims=True)
    centered = values - row_average
    variance = jnp.mean(centered * centered, axis=1, keepdims=True)
    inverse_std = 1.0 / jnp.sqrt(variance + 1e-05)
    return (centered * inverse_std, inverse_std)


def wrap(index, n):
    return index & (n - 1) if n & (n - 1) == 0 else lax.rem(index, n)


def ring_order(n):
    if n % 2:
        return list(range(n))
    return list(range(0, n, 2)) + list(range(n - 1, 0, -2))


def after(value, *others):
    return lax.optimization_barrier((value,) + others)[0]


def call(body, outs, *operands, limit=40):
    return pl.pallas_call(
        body,
        out_shape=[jax.ShapeDtypeStruct(s, t) for s, t in outs],
        in_specs=[VMEM] * len(operands),
        out_specs=[VMEM] * len(outs),
        compiler_params=pltpu.CompilerParams(vmem_limit_bytes=limit << 20),
    )(*operands)


def slots_of(target, me, n, capacity):
    rows = target.shape[1]
    relative = jnp.where(target < me, target - me + n, target - me)
    relative = jnp.where(target < n, relative, n)
    across = jnp.broadcast_to(relative.astype(f32), (rows, rows))
    row = lax.broadcasted_iota(jnp.int32, (rows, rows), 0)
    column = lax.broadcasted_iota(jnp.int32, (rows, rows), 1)
    same = jnp.where((row < column) & (across == across.T), 1.0, 0.0)
    ranked = jnp.sum(same, axis=0, keepdims=True).astype(jnp.int32)
    return jnp.where(relative < n, relative * capacity + ranked, -1), row


def pack_body(n, target_ref, tokens_ref, cot_ref, *outs):
    rows, width = tokens_ref.shape
    capacity = rows // n
    slots, row = slots_of(target_ref[...], lax.axis_index("dp"), n, capacity)
    placing = jnp.where(slots == row, 1.0, 0.0).astype(bf16)
    for start, ref in ((0, tokens_ref), (width, cot_ref)):
        packed = jnp.dot(placing, ref[...], preferred_element_type=f32).astype(bf16)
        for k, out in enumerate(outs):
            out[:, start : start + width] = packed[k * capacity : (k + 1) * capacity]


def collect_body(n, gain_ref, *refs):
    blocks, (packed_in, packed_cot, normed) = refs[:n], refs[n:]
    capacity, width = blocks[0].shape[0], packed_in.shape[1]
    me = lax.axis_index("dp")
    for k, block in enumerate(blocks):
        source = jnp.where(me < k, me - k + n, me - k)
        rows = pl.ds(pl.multiple_of(source * capacity, capacity), capacity)
        packed_in[rows, :] = block[:, :width]
        packed_cot[rows, :] = block[:, width:]
    standardized, _ = apply_layer_norm(packed_in[...].astype(f32))
    normed[...] = (standardized * gain_ref[...]).astype(bf16)


def forward_body(normed_ref, weight_ref, bias_ref, act_ref, slope_ref):
    hidden = weight_ref.shape[1]
    tile = min(256, hidden)
    for start in range(0, hidden, tile):
        cols = slice(start, start + tile)
        pre = jnp.dot(normed_ref[...], weight_ref[:, cols], preferred_element_type=f32)
        act, slope = gelu_pair(pre + bias_ref[:, cols])
        act_ref[:, cols] = act.astype(bf16)
        slope_ref[:, cols] = slope


def backward_body(cot_ref, weight_ref, slope_ref, grad_ref, bias_ref):
    hidden = weight_ref.shape[0]
    tile = min(256, hidden)
    for start in range(0, hidden, tile):
        cols = slice(start, start + tile)
        act_grad = lax.dot_general(
            cot_ref[...], weight_ref[cols, :], (((1,), (1,)), ((), ())), preferred_element_type=f32
        )
        grad = (act_grad * slope_ref[:, cols]).astype(bf16)
        grad_ref[:, cols] = grad
        bias_ref[:, cols] = jnp.sum(grad.astype(f32), axis=0, keepdims=True)


def fsdp_steps(n):
    if n % 2:
        return [lambda i, k=k: (i + k) % n for k in range(n)]
    return [lambda i, k=k: (i + 2 * k) % n for k in range(n // 2)] + [
        lambda i, k=k: ((i ^ 1) + 2 * k) % n for k in range(n // 2)
    ]


def gather_rows(own, n):
    owners = fsdp_steps(n)
    if n % 2:
        return [own] + [
            lax.ppermute(own, "fsdp", [(owner(i), i) for i in range(n)]) for owner in owners[1:]
        ]
    held = [own] + [
        lax.ppermute(own, "fsdp", [(owner(i), i) for i in range(n)]) for owner in owners[1 : n // 2]
    ]
    return held + [lax.ppermute(h, "fsdp", [(i, i ^ 1) for i in range(n)]) for h in held]


def butterfly_step(value, axis, step):
    n = lax.axis_size(axis)
    return value + lax.ppermute(value, axis, [(i, i ^ step) for i in range(n)])


def shards(tokens, cotangent, routes, norm_gain_vector, up_weight, up_bias, down_weight):
    slots, width = tokens.shape
    hidden = up_weight.shape[1]
    n = lax.axis_size("dp")
    fsdp_size = lax.axis_size("fsdp")
    capacity = slots // n
    me = lax.axis_index("dp")
    target = routes.reshape(1, slots)
    gain_row = norm_gain_vector.reshape(1, width)

    if capacity % 16 == 0:
        blocks = call(
            functools.partial(pack_body, n),
            [((capacity, 2 * width), bf16)] * n,
            target,
            tokens,
            cotangent,
        )
    else:
        index, row = slots_of(target, me, n, capacity)
        placing = (index == row).astype(bf16)
        both = jnp.concatenate([tokens, cotangent], axis=1)
        packed = jnp.dot(placing, both, preferred_element_type=f32).astype(bf16)
        blocks = [packed[k * capacity : (k + 1) * capacity] for k in range(n)]
    arrived = [blocks[0]] + [
        lax.ppermute(blocks[k], "dp", [(i, (i + k) % n) for i in range(n)]) for k in range(1, n)
    ]
    if capacity % 16 == 0:
        packed_in, packed_cot, normed_own = call(
            functools.partial(collect_body, n),
            [((slots, width), bf16)] * 3,
            gain_row,
            *arrived,
        )
    else:
        order = jnp.mod(me - jnp.arange(n), n)
        packed = jnp.take(jnp.stack(arrived), order, axis=0).reshape(slots, 2 * width)
        packed_in, packed_cot = packed[:, :width], packed[:, width:]
        normed_own = (apply_layer_norm(packed_in.astype(f32))[0] * gain_row).astype(bf16)

    normed = jnp.concatenate(gather_rows(normed_own, fsdp_size), axis=0)
    all_cot = jnp.concatenate(gather_rows(packed_cot, fsdp_size), axis=0)
    rows = normed.shape[0]
    act, slope = call(
        forward_body,
        [((rows, hidden), bf16), ((rows, hidden), f32)],
        normed,
        up_weight,
        up_bias.reshape(1, hidden),
    )

    order = ring_order(n)
    if n % 2:
        here = me
    else:
        here = jnp.where(me & 1 == 1, n - 1 - (me >> 1), me >> 1)
    forward = [(order[i], order[(i + 1) % n]) for i in range(n)]
    backward = [(order[i], order[i - 1]) for i in range(n)]
    ways = ((1, forward), (-1, backward))

    def own_part(lhs, rhs, way, step):
        columns = rhs.shape[1] // 2
        half = rhs[:, :columns] if way > 0 else rhs[:, columns:]
        count = lhs.shape[1] // n
        piece = wrap(here + 2 * n - way * (step + 1), n)
        block = lax.dynamic_slice_in_dim(lhs, piece * count, count, 1)
        return lax.dot_general(block, half, (((0,), (0,)), ((), ())), preferred_element_type=f32)

    down = [own_part(act, all_cot, way, 0).astype(bf16) for way, _ in ways]
    cot_later = after(all_cot, *down)
    pre_grad, bias_part = call(
        backward_body,
        [((rows, hidden), bf16), ((1, hidden), f32)],
        cot_later,
        down_weight,
        slope,
    )
    up = [own_part(normed, pre_grad, way, 0).astype(bf16) for way, _ in ways]
    totals = down + up
    factors = [(act, all_cot)] * 2 + [(normed, pre_grad)] * 2
    owners = fsdp_steps(fsdp_size)
    sent = [None] * fsdp_size
    for step in range(n - 1):
        for i in range(4):
            way, perm = ways[i % 2]
            lhs, rhs = factors[i]
            moved = lax.ppermute(totals[i], "dp", perm)
            part = own_part(after(lhs, totals[i]), rhs, way, step + 1)
            totals[i] = (moved.astype(f32) + part).astype(bf16)
        if step == 0:
            partial = lax.dot_general(
                after(pre_grad, totals[0]),
                up_weight,
                (((1,), (1,)), ((), ())),
                preferred_element_type=f32,
            ).astype(bf16)
            sent[0] = partial[:slots]
        if step > 0:
            per_step = -(-(fsdp_size - 1) // (n - 2)) if n > 2 else fsdp_size
            for k in range(1 + (step - 1) * per_step, min(fsdp_size, 1 + step * per_step)):
                block = after(partial[k * slots : (k + 1) * slots], totals[2])
                sent[k] = lax.ppermute(
                    block, "fsdp", [(i, owners[k](i)) for i in range(fsdp_size)]
                )
    normed_gradient = sum(s.astype(f32) for s in sent)
    standardized, inverse_std = apply_layer_norm(packed_in.astype(f32))
    gain_part = jnp.sum(normed_gradient * standardized, axis=0)
    scaled = normed_gradient * norm_gain_vector
    input_grad = packed_cot.astype(f32) + inverse_std * (
        scaled
        - jnp.mean(scaled, axis=1, keepdims=True)
        - standardized * jnp.mean(scaled * standardized, axis=1, keepdims=True)
    )

    small_steps = [("fsdp", 1 << k) for k in range((fsdp_size - 1).bit_length())]
    small_steps += [("dp", 1 << k) for k in range((n - 1).bit_length())]
    small = gain_part
    results = [jnp.zeros((hidden, width), f32), jnp.zeros((width, hidden), f32)]

    def put(i, piece, values):
        count, columns = values.shape
        results[i // 2] = lax.dynamic_update_slice(
            results[i // 2], values.astype(f32), (piece * count, columns * (i % 2))
        )

    for i in range(4):
        put(i, here, totals[i])
    for step in range(n - 1):
        for i in range(4):
            way, perm = ways[i % 2]
            totals[i] = lax.ppermute(totals[i], "dp", perm)
            put(i, wrap(here + n - way * (step + 1), n), totals[i])
        if step < len(small_steps) or step == n - 2:
            last = len(small_steps) if step == n - 2 else step + 1
            for axis, distance in small_steps[step:last]:
                if axis == "dp" and small.shape[0] == width:
                    small = jnp.concatenate([small, bias_part[0]])
                small = butterfly_step(after(small, totals[2]), axis, distance)
    down_grad, up_grad = results
    gain_grad, bias_grad = small[:width], small[width:]
    return (input_grad.astype(bf16), up_grad, bias_grad, down_grad, gain_grad)


def solution(mesh):
    return jax.shard_map(
        shards,
        mesh=mesh,
        in_specs=(
            P(("dp", "fsdp"), None),
            P(("dp", "fsdp"), None),
            P(("dp", "fsdp"), None),
            P(),
            P(None, "fsdp"),
            P("fsdp"),
            P("fsdp", None),
        ),
        out_specs=(P(("dp", "fsdp"), None), P(None, "fsdp"), P("fsdp"), P("fsdp", None), P()),
        check_vma=False,
    )
```

```python
import functools

import jax
import jax.numpy as jnp
from jax import lax
from jax.experimental import pallas as pl
from jax.experimental.pallas import tpu as pltpu
from jax.sharding import PartitionSpec as P

root_two_pi = 0.7978845608
cubic = 0.044715
f32 = jnp.float32
bf16 = jnp.bfloat16
VMEM = pl.BlockSpec(memory_space=pltpu.VMEM)


def gelu_pair(pre):
    inner = root_two_pi * (pre + cubic * pre * pre * pre)
    tangent = jnp.tanh(inner)
    act = 0.5 * pre * (1.0 + tangent)
    slope = 0.5 * (1.0 + tangent) + 0.5 * pre * (1.0 - tangent * tangent) * root_two_pi * (
        1.0 + 3.0 * cubic * pre * pre
    )
    return (act, slope)


def apply_layer_norm(values):
    row_average = jnp.mean(values, axis=1, keepdims=True)
    centered = values - row_average
    variance = jnp.mean(centered * centered, axis=1, keepdims=True)
    inverse_std = 1.0 / jnp.sqrt(variance + 1e-05)
    return (centered * inverse_std, inverse_std)


def after(value, *others):
    return lax.optimization_barrier((value,) + others)[0]


def call(body, outs, *operands, limit=40):
    return pl.pallas_call(
        body,
        out_shape=[jax.ShapeDtypeStruct(s, t) for s, t in outs],
        in_specs=[VMEM] * len(operands),
        out_specs=[VMEM] * len(outs),
        compiler_params=pltpu.CompilerParams(vmem_limit_bytes=limit << 20),
    )(*operands)


def slots_of(target, me, n, capacity):
    rows = target.shape[1]
    relative = jnp.where(target < me, target - me + n, target - me)
    relative = jnp.where(target < n, relative, n)
    across = jnp.broadcast_to(relative.astype(f32), (rows, rows))
    row = lax.broadcasted_iota(jnp.int32, (rows, rows), 0)
    column = lax.broadcasted_iota(jnp.int32, (rows, rows), 1)
    same = jnp.where((row < column) & (across == across.T), 1.0, 0.0)
    ranked = jnp.sum(same, axis=0, keepdims=True).astype(jnp.int32)
    return jnp.where(relative < n, relative * capacity + ranked, -1), row


def pack_body(n, target_ref, tokens_ref, cot_ref, *outs):
    rows, width = tokens_ref.shape
    capacity = rows // n
    slots, row = slots_of(target_ref[...], lax.axis_index("dp"), n, capacity)
    placing = jnp.where(slots == row, 1.0, 0.0).astype(bf16)
    for start, ref in ((0, tokens_ref), (width, cot_ref)):
        packed = jnp.dot(placing, ref[...], preferred_element_type=f32).astype(bf16)
        for k, out in enumerate(outs):
            out[:, start : start + width] = packed[k * capacity : (k + 1) * capacity]


def collect_body(n, gain_ref, *refs):
    blocks, (packed_in, packed_cot, normed) = refs[:n], refs[n:]
    capacity, width = blocks[0].shape[0], packed_in.shape[1]
    me = lax.axis_index("dp")
    for k, block in enumerate(blocks):
        source = jnp.where(me < k, me - k + n, me - k)
        rows = pl.ds(pl.multiple_of(source * capacity, capacity), capacity)
        packed_in[rows, :] = block[:, :width]
        packed_cot[rows, :] = block[:, width:]
    standardized, _ = apply_layer_norm(packed_in[...].astype(f32))
    normed[...] = (standardized * gain_ref[...]).astype(bf16)


def forward_body(normed_ref, weight_ref, bias_ref, act_ref, slope_ref):
    hidden = weight_ref.shape[1]
    tile = min(256, hidden)
    for start in range(0, hidden, tile):
        cols = slice(start, start + tile)
        pre = jnp.dot(normed_ref[...], weight_ref[:, cols], preferred_element_type=f32)
        act, slope = gelu_pair(pre + bias_ref[:, cols])
        act_ref[:, cols] = act.astype(bf16)
        slope_ref[:, cols] = slope


def backward_body(cot_ref, weight_ref, slope_ref, grad_ref, bias_ref):
    hidden = weight_ref.shape[0]
    tile = min(256, hidden)
    for start in range(0, hidden, tile):
        cols = slice(start, start + tile)
        act_grad = lax.dot_general(
            cot_ref[...], weight_ref[cols, :], (((1,), (1,)), ((), ())), preferred_element_type=f32
        )
        grad = (act_grad * slope_ref[:, cols]).astype(bf16)
        grad_ref[:, cols] = grad
        bias_ref[:, cols] = jnp.sum(grad.astype(f32), axis=0, keepdims=True)


def fsdp_steps(n):
    if n % 2:
        return [lambda i, k=k: (i + k) % n for k in range(n)]
    return [lambda i, k=k: (i + 2 * k) % n for k in range(n // 2)] + [
        lambda i, k=k: ((i ^ 1) + 2 * k) % n for k in range(n // 2)
    ]


def gather_rows(own, n, first=lambda h: h):
    owners = fsdp_steps(n)
    if n % 2:
        return [own] + [
            lax.ppermute(own, "fsdp", [(owner(i), i) for i in range(n)]) for owner in owners[1:]
        ]
    held = [own] + [
        lax.ppermute(own, "fsdp", [(owner(i), i) for i in range(n)]) for owner in owners[1 : n // 2]
    ]
    later = held[:1] + [first(h) for h in held[1:]]
    return held + [lax.ppermute(h, "fsdp", [(i, i ^ 1) for i in range(n)]) for h in later]


def butterfly_step(value, axis, step):
    n = lax.axis_size(axis)
    return value + lax.ppermute(value, axis, [(i, i ^ step) for i in range(n)])


def shards(tokens, cotangent, routes, norm_gain_vector, up_weight, up_bias, down_weight):
    slots, width = tokens.shape
    hidden = up_weight.shape[1]
    n = lax.axis_size("dp")
    fsdp_size = lax.axis_size("fsdp")
    capacity = slots // n
    me = lax.axis_index("dp")
    target = routes.reshape(1, slots)
    gain_row = norm_gain_vector.reshape(1, width)

    if capacity % 16 == 0:
        blocks = call(
            functools.partial(pack_body, n),
            [((capacity, 2 * width), bf16)] * n,
            target,
            tokens,
            cotangent,
        )
    else:
        index, row = slots_of(target, me, n, capacity)
        placing = (index == row).astype(bf16)
        both = jnp.concatenate([tokens, cotangent], axis=1)
        packed = jnp.dot(placing, both, preferred_element_type=f32).astype(bf16)
        blocks = [packed[k * capacity : (k + 1) * capacity] for k in range(n)]
    up_weight, down_weight = after(up_weight, blocks[0]), after(down_weight, blocks[0])
    arrived = [blocks[0]] + [
        lax.ppermute(blocks[k], "dp", [(i, (i + k) % n) for i in range(n)]) for k in range(1, n)
    ]
    if capacity % 16 == 0:
        packed_in, packed_cot, normed_own = call(
            functools.partial(collect_body, n),
            [((slots, width), bf16)] * 3,
            gain_row,
            *arrived,
        )
    else:
        order = jnp.mod(me - jnp.arange(n), n)
        packed = jnp.take(jnp.stack(arrived), order, axis=0).reshape(slots, 2 * width)
        packed_in, packed_cot = packed[:, :width], packed[:, width:]
        normed_own = (apply_layer_norm(packed_in.astype(f32))[0] * gain_row).astype(bf16)

    normed = jnp.concatenate(gather_rows(normed_own, fsdp_size), axis=0)
    rows = normed.shape[0]
    act, slope = call(
        forward_body,
        [((rows, hidden), bf16), ((rows, hidden), f32)],
        normed,
        up_weight,
        up_bias.reshape(1, hidden),
    )
    all_cot = gather_rows(packed_cot, fsdp_size, lambda h: after(h, act))
    all_cot = jnp.concatenate(all_cot, axis=0)

    bits = (n - 1).bit_length()
    y_first = list(range(bits))
    z_first = y_first[1:2] + y_first[:1] + y_first[2:]

    def exchange(value, bit):
        return lax.ppermute(value, "dp", [(i, i ^ (1 << bit)) for i in range(n)])

    def own_bit(bit):
        return (me >> bit) & 1

    def product(lhs, rhs, start, count):
        block = lax.dynamic_slice_in_dim(lhs, start, count, 1)
        return lax.dot_general(block, rhs, (((0,), (0,)), ((), ())), preferred_element_type=f32)

    class Chunk:
        def __init__(self, lhs, rhs, index, parts, order):
            self.count = lhs.shape[1] // parts
            self.base = index * self.count
            self.lhs, self.rhs, self.order = lhs, rhs, order
            self.keep, self.moved = None, None
            self.offset = 0

        def first(self):
            half = self.count // 2
            mine = own_bit(self.order[0])
            send = product(self.lhs, self.rhs, self.base + (1 - mine) * half, half).astype(bf16)
            self.moved = exchange(send, self.order[0])
            keep = product(self.lhs, self.rhs, self.base + mine * half, half)
            self.keep = after(keep, send)
            self.offset = mine * half
            self.length = half

        def halve(self, step):
            half = self.length // 2
            mine = own_bit(self.order[step])
            out = []
            for start in ((1 - mine) * half, mine * half):
                k = lax.dynamic_slice_in_dim(self.keep, start, half, 0).astype(f32)
                m = lax.dynamic_slice_in_dim(self.moved, start, half, 0).astype(f32)
                out.append((k + m).astype(bf16))
            self.moved = exchange(out[0], self.order[step])
            self.keep = out[1]
            self.offset = self.offset + mine * half
            self.length = half

        def total(self):
            self.held = (self.keep.astype(f32) + self.moved.astype(f32)).astype(bf16)
            self.step = len(self.order) - 1

        def spread(self):
            mine = own_bit(self.order[self.step])
            moved = exchange(self.held, self.order[self.step])
            if self.step == 0:
                return [(self.held, self.offset), (moved, self.offset + (1 - 2 * mine) * self.length)]
            three = jnp.zeros((2 * self.length, self.held.shape[1]), bf16)
            three = lax.dynamic_update_slice(three, self.held, (mine * self.length, 0))
            three = lax.dynamic_update_slice(three, moved, ((1 - mine) * self.length, 0))
            self.held = three
            self.offset = self.offset - mine * self.length
            self.length *= 2
            self.step -= 1

    down = [Chunk(act, all_cot, 0, 2, y_first), Chunk(act, all_cot, 1, 2, z_first)]
    for chunk in down:
        chunk.first()
    pre_grad, bias_part = call(
        backward_body,
        [((rows, hidden), bf16), ((1, hidden), f32)],
        all_cot,
        down_weight,
        slope,
    )
    up = [Chunk(normed, pre_grad, 0, 2, y_first), Chunk(normed, pre_grad, 1, 2, y_first)]
    up[0].first()
    if bits > 1:
        down[1].halve(1)
        up[1].lhs = after(normed, down[1].keep)
    up[1].first()

    owners = fsdp_steps(fsdp_size)
    partial = lax.dot_general(
        pre_grad, up_weight, (((1,), (1,)), ((), ())), preferred_element_type=f32
    ).astype(bf16)
    normed_gradient = partial[:slots].astype(f32)
    for k in range(1, fsdp_size):
        moved = lax.ppermute(
            partial[k * slots : (k + 1) * slots],
            "fsdp",
            [(i, owners[k](i)) for i in range(fsdp_size)],
        )
        normed_gradient = normed_gradient + moved.astype(f32)
    standardized, inverse_std = apply_layer_norm(packed_in.astype(f32))
    gain_part = jnp.sum(normed_gradient * standardized, axis=0)
    scaled = normed_gradient * norm_gain_vector
    input_grad = packed_cot.astype(f32) + inverse_std * (
        scaled
        - jnp.mean(scaled, axis=1, keepdims=True)
        - standardized * jnp.mean(scaled * standardized, axis=1, keepdims=True)
    )
    small = gain_part
    for k in range((fsdp_size - 1).bit_length()):
        small = butterfly_step(small, "fsdp", 1 << k)
    small = jnp.concatenate([small, bias_part[0]])
    for k in range(bits):
        small = butterfly_step(small, "dp", 1 << k)

    chunks = [down[0], up[0], down[1], up[1]]
    for chunk in chunks:
        for step in range(2 if chunk is down[1] else 1, bits):
            chunk.halve(step)
        chunk.total()
    results = []
    for pair in (down, up):
        result = jnp.zeros((2 * pair[0].count, pair[0].rhs.shape[1]), f32)
        for chunk in pair:
            placed = None
            while placed is None:
                placed = chunk.spread()
            for values, offset in placed:
                result = lax.dynamic_update_slice(
                    result, values.astype(f32), (chunk.base + offset, 0)
                )
        results.append(result)
    down_grad, up_grad = results
    gain_grad, bias_grad = small[:width], small[width:]
    return (input_grad.astype(bf16), up_grad, bias_grad, down_grad, gain_grad)


def solution(mesh):
    return jax.shard_map(
        shards,
        mesh=mesh,
        in_specs=(
            P(("dp", "fsdp"), None),
            P(("dp", "fsdp"), None),
            P(("dp", "fsdp"), None),
            P(),
            P(None, "fsdp"),
            P("fsdp"),
            P("fsdp", None),
        ),
        out_specs=(P(("dp", "fsdp"), None), P(None, "fsdp"), P("fsdp"), P("fsdp", None), P()),
        check_vma=False,
    )
```
